32 devices in a mesh: doc: 4 (over y, core), term: 8 (over z, x).
Axes of the slice: x: 2, y: 2, z: 4, core: 2. Of those that a mesh axis runs over, the one named last changes fastest.
Arguments:
- slab: float32 [4096, 8192], P('doc', 'term'), may hold values from 0.05 to 4
- doc_factor: float32 [4096, 128], P('doc'), may hold values from 0.02 to 5, as said below
- term_factor: float32 [8192, 128], P('term'), may hold values from 0.005 to 5, as said below
Outputs:
- doc_out: float32 [4096, 128], P('doc')
- term_out: float32 [8192, 128], P('term')
The draws below stay inside these ranges and needn't reach their ends.
Inputs may be any that keep to these rules, and one draw needn't show every extreme that they name: `doc_factor`: positive entries. `term_factor`: positive entries.
All inputs are finite; a program needn't handle non-finite values.
Results may differ from the reference program's by a relative error of at most 0.0001.
Values sent between devices are 32-bit elements; how exact they have to be, the bound alone decides.
A program may use at most 64 MiB of HBM per device.

```python
import math
import jax
import jax.numpy as jnp
from jax import lax

RANK = 128
OUTER = 2
INNER = 2
DOCS = 4096
TERMS = 8192


def peaked_rows(key, count, width, low, high):
    first = jax.random.fold_in(key, 1)
    second = jax.random.fold_in(key, 2)
    third = jax.random.fold_in(key, 3)
    base = jnp.exp(jax.random.uniform(first, (count, width), jnp.float32, math.log(low), math.log(high)))
    peak = jnp.exp(jax.random.uniform(third, (count,), jnp.float32, 0.0, math.log(5.0)))
    topic = jax.random.randint(second, (count,), 0, width)
    chosen = jnp.arange(width)[None, :] == topic[:, None]
    return jnp.where(chosen, peak[:, None], base).astype(jnp.float32)


def draw_doc_factor(key, part):
    return peaked_rows(jax.random.fold_in(key, 11), DOCS, RANK, 0.02, 0.2)


def draw_term_factor(key, part):
    return peaked_rows(jax.random.fold_in(key, 23), TERMS, RANK, 0.005, 0.05)


def shard_levels(rng, extent, shards, low, largest):
    level, own = 1.0, jax.random.fold_in(rng, 6)
    for axis_at, blocks in shards:
        draws = jnp.exp(jax.random.uniform(jax.random.fold_in(own, axis_at), (blocks,), jnp.float32, low / len(shards), largest / len(shards)))
        level = level * jnp.repeat(draws, extent[axis_at] // blocks).reshape([-1 if axis == axis_at else 1 for axis in range(len(extent))])
    return level


def setup_inputs(seed: int = 0) -> dict:
    keys = jax.random.split(jax.random.key(seed), 4)
    return {
        "slab": jnp.clip(jnp.exp(math.log(4.0) - 4.3820266 * jax.random.uniform(keys[0], (DOCS, TERMS), jnp.float32) ** shard_levels(keys[0], (DOCS, TERMS), ((0, 4), (1, 8)), -0.2, 0.2)), 0.05, 4.0),
        "doc_factor": draw_doc_factor(jax.random.fold_in(keys[3], 71), 0),
        "term_factor": draw_term_factor(jax.random.fold_in(keys[3], 71), 0),
    }


def quotient(slab, doc_factor, term_factor):
    product = jnp.dot(doc_factor, term_factor.T, precision=lax.Precision.HIGHEST, preferred_element_type=jnp.float32)
    return slab / product


def reference(slab, doc_factor, term_factor):
    for _ in range(OUTER):
        for _ in range(INNER):
            ratios = quotient(slab, doc_factor, term_factor)
            numerator = jnp.dot(ratios, term_factor, precision=lax.Precision.HIGHEST, preferred_element_type=jnp.float32)
            doc_factor = doc_factor * numerator / jnp.sum(term_factor, axis=0)
        ratios = quotient(slab, doc_factor, term_factor)
        numerator = jnp.dot(ratios.T, doc_factor, precision=lax.Precision.HIGHEST, preferred_element_type=jnp.float32)
        term_factor = term_factor * numerator / jnp.sum(doc_factor, axis=0)
    return doc_factor, term_factor
```

```python
import functools

import jax
import jax.numpy as jnp
from jax import lax
from jax.experimental import pallas as pl
from jax.experimental.pallas import tpu as pltpu
from jax.sharding import PartitionSpec as P

OUTER = 2
INNER = 2
TILE = 256
DOC_CHUNKS = 4
TERM_CHUNKS = 2
MESH = pl.DeviceIdType.MESH
F32 = jnp.float32
BF16 = jnp.bfloat16


def halves(x):
    high = x.astype(BF16)
    return high, (x - high.astype(F32)).astype(BF16)


def dot(a, b, dims=((1,), (0,))):
    return lax.dot_general(a, b, (dims, ((), ())), preferred_element_type=F32)


def fold(x):
    rows, cols = x.shape
    return jnp.sum(x.reshape(rows // 8, 8, cols), axis=0)


class Group:
    def __init__(self, axis, size):
        self.axis, self.size = axis, size
        self.outer = size // 2
        self.me = lax.axis_index(axis)
        self.x = lax.rem(self.me, 2)
        self.z = lax.div(self.me, 2)
        self.pair = {axis: self.me + 1 - 2 * self.x}

    def place(self, d):
        return lax.rem(self.z + d, self.outer)

    def peer(self, d):
        return {self.axis: self.place(d) * 2 + self.x}

    def everyone(self):
        return [self.pair] + [self.peer(d) for d in range(1, self.outer)]


class Reduce:
    def __init__(self, group, rows, part, r1, acc, r2, send, recv):
        self.g, self.rows = group, rows
        self.half, self.own = rows // 2, rows // 2 // group.outer
        self.part, self.r1, self.acc, self.r2 = part, r1, acc, r2
        self.send, self.recv = send, recv

    def copy(self, src, dst, stage, device):
        return pltpu.make_async_remote_copy(
            src_ref=src, dst_ref=dst, send_sem=self.send.at[stage], recv_sem=self.recv.at[stage],
            device_id=device, device_id_type=MESH)

    def many(self, sem):
        pltpu.make_async_copy(self.r2, self.r2, sem).wait()

    def half_at(self, x):
        return pl.multiple_of(x * self.half, 8)

    def s1(self):
        self.c1 = self.copy(self.part.at[pl.ds(self.half_at(1 - self.g.x), self.half)], self.r1, 0, self.g.pair)
        self.c1.start()

    def s2(self):
        self.c1.wait()
        self.acc[...] = self.part[pl.ds(self.half_at(self.g.x), self.half)] + self.r1[...]
        for d in range(1, self.g.outer):
            at = pl.multiple_of(self.g.place(d) * self.own, 8)
            self.copy(self.acc.at[pl.ds(at, self.own)], self.r2.at[d - 1], 1, self.g.peer(d)).start()

    def s3(self, base, old, new, mass):
        self.new, self.base = new, base
        if self.g.outer > 1:
            self.many(self.recv.at[1])
        total = self.acc[pl.ds(pl.multiple_of(self.g.z * self.own, 8), self.own)]
        for d in range(self.g.outer - 1):
            total = total + self.r2[d]
        at = pl.multiple_of(base + self.half_at(self.g.x) + self.g.z * self.own, 8)
        rows = pl.ds(at, self.own)
        new[rows] = old[rows] * total / mass()
        for d in range(1, self.g.outer):
            self.copy(new.at[rows], new.at[rows], 2, self.g.peer(d)).start()

    def s4(self):
        if self.g.outer > 1:
            self.many(self.recv.at[2])
            self.many(self.send.at[1])
        rows = pl.ds(pl.multiple_of(self.base + self.half_at(self.g.x), 8), self.half)
        self.c4 = self.copy(self.new.at[rows], self.new.at[rows], 3, self.g.pair)
        self.c4.start()

    def s5(self):
        self.c4.wait()
        if self.g.outer > 1:
            self.many(self.send.at[2])


class Mass:
    def __init__(self, group, buf, got, send, recv):
        self.g, self.buf, self.got, self.send, self.recv = group, buf, got, send, recv

    def copy(self, src, dst, stage, device):
        return pltpu.make_async_remote_copy(
            src_ref=src, dst_ref=dst, send_sem=self.send.at[stage], recv_sem=self.recv.at[stage],
            device_id=device, device_id_type=MESH)

    def s1(self, value):
        self.buf[0] = value
        self.c1 = self.copy(self.buf.at[0], self.got.at[0], 0, self.g.pair)
        self.c1.start()

    def s2(self):
        self.c1.wait()
        self.buf[1] = self.buf[0] + self.got[0]
        for d in range(1, self.g.outer):
            self.copy(self.buf.at[1], self.got.at[d], 1, self.g.peer(d)).start()

    def s3(self):
        total = self.buf[1]
        if self.g.outer > 1:
            rest = self.got.at[pl.ds(1, self.g.outer - 1)]
            pltpu.make_async_copy(rest, rest, self.recv.at[1]).wait()
            pltpu.make_async_copy(rest, rest, self.send.at[1]).wait()
            for d in range(1, self.g.outer):
                total = total + self.got[d]
        self.buf[2] = jnp.broadcast_to(jnp.sum(total, axis=0, keepdims=True), total.shape)

    def value(self):
        return self.buf[2, 0:1]


def kernel(docs_axis, terms_axis, slab, h_in, w_in, h_out, w_out,
           hbuf, wbuf, wk, tt,
           dpart, dr1, dacc, dr2, dsend, drecv,
           tpart, tr1, tacc, tr2, tsend, trecv,
           mbuf, mgot, msend, mrecv, cbuf, cgot, csend, crecv):
    docs, terms = slab.shape
    rank = h_in.shape[1]
    gt, gd = Group(*terms_axis), Group(*docs_axis)
    peers = gt.everyone() + gd.everyone()
    barrier = pltpu.get_barrier_semaphore()
    for device in peers:
        pl.semaphore_signal(barrier, inc=1, device_id=device, device_id_type=MESH)
    pl.semaphore_wait(barrier, len(peers))

    chunk, tchunk = docs // DOC_CHUNKS, terms // TERM_CHUNKS
    tile = min(TILE, terms)

    def quotients(h, rows):
        high, low = halves(h)
        lhs = jnp.concatenate([high, low, high], axis=1)
        for t in range(0, terms, tile):
            product = dot(lhs, wk[t:t + tile], ((1,), (1,)))
            yield t, halves(slab[rows, t:t + tile] / product)

    def doc_partial(h, c, out):
        both, one = None, None
        for t, (high, low) in quotients(h, slice(c * chunk, (c + 1) * chunk)):
            b = dot(high, wk[t:t + tile, rank:])
            o = dot(low, wk[t:t + tile, :rank])
            both, one = (b, o) if both is None else (both + b, one + o)
        out[...] = both[:, :rank] + both[:, rank:] + one

    def term_partial(h, c):
        high_t, low_t = halves(h.T)
        lhs = jnp.concatenate([high_t, low_t], axis=0)
        for t, (high, low) in quotients(h, slice(c * chunk, (c + 1) * chunk)):
            b = dot(lhs, high)
            value = b[:rank] + b[rank:] + dot(high_t, low)
            if c > 0:
                value = value + tt[:, t:t + tile]
            tt[:, t:t + tile] = value

    for o in range(OUTER):
        w_old = w_in if o == 0 else wbuf.at[o - 1]
        w_new = w_out if o == OUTER - 1 else wbuf.at[o]
        w = w_old[...]
        high, low = halves(w)
        wk[:, :rank] = high
        wk[:, rank:2 * rank] = high
        wk[:, 2 * rank:] = low
        mass = Mass(gt, mbuf.at[o], mgot.at[o], msend.at[o], mrecv.at[o])
        mass.s1(fold(w))

        def h_ref(u):
            if u == 0:
                return h_in
            return h_out if u == OUTER * INNER else hbuf.at[u - 1]

        jobs = []
        count = INNER * DOC_CHUNKS
        doc_mass = None
        for j in range(count + DOC_CHUNKS):
            u, c = o * INNER + j // DOC_CHUNKS, j % DOC_CHUNKS
            rows = slice(c * chunk, (c + 1) * chunk)
            if j >= DOC_CHUNKS:
                jobs[j - DOC_CHUNKS].s5()
            h = h_ref(u)[rows]
            if j < count:
                doc_partial(h, c, dpart.at[u, c])
                job = Reduce(gt, chunk, dpart.at[u, c], dr1.at[u, c], dacc.at[u, c], dr2.at[u, c],
                             dsend.at[u, c], drecv.at[u, c])
                job.u, job.c = u, c
                jobs.append(job)
                job.s1()
            else:
                doc_mass = fold(h) if doc_mass is None else doc_mass + fold(h)
                term_partial(h, c)
            if j == 1:
                mass.s2()
            if j == 2:
                mass.s3()
            if 1 <= j <= count:
                jobs[j - 1].s2()
            if 2 <= j <= count + 1:
                k = jobs[j - 2]
                k.s3(k.c * chunk, h_ref(k.u), h_ref(k.u + 1), mass.value)
            if 3 <= j <= count + 2:
                jobs[j - 3].s4()

        sums = Mass(gd, cbuf.at[o], cgot.at[o], csend.at[o], crecv.at[o])
        sums.s1(doc_mass)
        jobs = []
        for c in range(TERM_CHUNKS):
            tpart[o, c] = tt[:, c * tchunk:(c + 1) * tchunk].T
            job = Reduce(gd, tchunk, tpart.at[o, c], tr1.at[o, c], tacc.at[o, c], tr2.at[o, c],
                         tsend.at[o, c], trecv.at[o, c])
            jobs.append(job)
            job.s1()
        sums.s2()
        for job in jobs:
            job.s2()
        sums.s3()
        for c, job in enumerate(jobs):
            job.s3(c * tchunk, w_old, w_new, sums.value)
        for job in jobs:
            job.s4()
        for job in jobs:
            job.s5()


def solution(mesh):
    n, m = mesh.shape["term"], mesh.shape["doc"]

    def on_device(slab, h, w):
        docs, rank = h.shape
        terms = w.shape[0]
        chunk, tchunk = docs // DOC_CHUNKS, terms // TERM_CHUNKS
        vmem = pl.BlockSpec(memory_space=pltpu.VMEM)
        updates = OUTER * INNER

        def reduce_scratch(lead, rows, size):
            outer = size // 2
            half = rows // 2
            return [
                pltpu.VMEM(lead + (rows, rank), F32),
                pltpu.VMEM(lead + (half, rank), F32),
                pltpu.VMEM(lead + (half, rank), F32),
                pltpu.VMEM(lead + (max(outer - 1, 1), half // outer, rank), F32),
                pltpu.SemaphoreType.DMA(lead + (4,)),
                pltpu.SemaphoreType.DMA(lead + (4,)),
            ]

        def mass_scratch(size):
            return [
                pltpu.VMEM((OUTER, 3, 8, rank), F32),
                pltpu.VMEM((OUTER, size // 2, 8, rank), F32),
                pltpu.SemaphoreType.DMA((OUTER, 2)),
                pltpu.SemaphoreType.DMA((OUTER, 2)),
            ]

        return pl.pallas_call(
            functools.partial(kernel, ("doc", m), ("term", n)),
            out_shape=[jax.ShapeDtypeStruct(h.shape, F32), jax.ShapeDtypeStruct(w.shape, F32)],
            in_specs=[vmem] * 3,
            out_specs=[vmem] * 2,
            scratch_shapes=[
                pltpu.VMEM((updates - 1, docs, rank), F32),
                pltpu.VMEM((max(OUTER - 1, 1), terms, rank), F32),
                pltpu.VMEM((terms, 3 * rank), BF16),
                pltpu.VMEM((rank, terms), F32),
                *reduce_scratch((updates, DOC_CHUNKS), chunk, n),
                *reduce_scratch((OUTER, TERM_CHUNKS), tchunk, m),
                *mass_scratch(n),
                *mass_scratch(m),
            ],
            compiler_params=pltpu.CompilerParams(
                collective_id=0, has_side_effects=True, vmem_limit_bytes=56 * 1024 * 1024),
            cost_estimate=pl.CostEstimate(
                flops=36 * 2 * docs * terms * rank, bytes_accessed=6 * docs * terms, transcendentals=0),
        )(slab, h, w)

    return jax.shard_map(
        on_device,
        mesh=mesh,
        in_specs=(P("doc", "term"), P("doc", None), P("term", None)),
        out_specs=(P("doc", None), P("term", None)),
        check_vma=False,
    )
```

```python
import functools

import jax
import jax.numpy as jnp
from jax import lax
from jax.experimental import pallas as pl
from jax.experimental.pallas import tpu as pltpu
from jax.sharding import PartitionSpec as P

OUTER = 2
INNER = 2
DOC_CHUNKS = 8
TERM_CHUNKS = 4
MESH = pl.DeviceIdType.MESH
F32 = jnp.float32
BF16 = jnp.bfloat16


def halves(x):
    high = x.astype(BF16)
    return high, (x - high.astype(F32)).astype(BF16)


def dot(a, b, dims=((1,), (0,))):
    return lax.dot_general(a, b, (dims, ((), ())), preferred_element_type=F32)


def fold(x):
    rows, cols = x.shape
    return jnp.sum(x.reshape(rows // 8, 8, cols), axis=0)


class Group:
    def __init__(self, axis, size):
        self.axis, self.size = axis, size
        self.outer = size // 2
        self.me = lax.axis_index(axis)
        self.x = lax.rem(self.me, 2)
        self.z = lax.div(self.me, 2)
        self.pair = {axis: self.me + 1 - 2 * self.x}

    def place(self, d):
        return lax.rem(self.z + d, self.outer)

    def peer(self, d):
        return {self.axis: self.place(d) * 2 + self.x}

    def everyone(self):
        return [self.pair] + [self.peer(d) for d in range(1, self.outer)]


class Reduce:
    def __init__(self, group, rows, part, r1, acc, r2, send, recv):
        self.g, self.rows = group, rows
        self.half, self.own = rows // 2, rows // 2 // group.outer
        self.part, self.r1, self.acc, self.r2 = part, r1, acc, r2
        self.send, self.recv = send, recv

    def copy(self, src, dst, stage, device):
        return pltpu.make_async_remote_copy(
            src_ref=src, dst_ref=dst, send_sem=self.send.at[stage], recv_sem=self.recv.at[stage],
            device_id=device, device_id_type=MESH)

    def many(self, sem):
        pltpu.make_async_copy(self.r2, self.r2, sem).wait()

    def half_at(self, x):
        return pl.multiple_of(x * self.half, 8)

    def s1(self):
        self.c1 = self.copy(self.part.at[pl.ds(self.half_at(1 - self.g.x), self.half)], self.r1, 0, self.g.pair)
        self.c1.start()

    def s2(self):
        self.c1.wait()
        self.acc[...] = self.part[pl.ds(self.half_at(self.g.x), self.half)] + self.r1[...]
        for d in range(1, self.g.outer):
            at = pl.multiple_of(self.g.place(d) * self.own, 8)
            self.copy(self.acc.at[pl.ds(at, self.own)], self.r2.at[d - 1], 1, self.g.peer(d)).start()

    def s3(self, base, old, new, mass):
        self.new, self.base = new, base
        if self.g.outer > 1:
            self.many(self.recv.at[1])
        total = self.acc[pl.ds(pl.multiple_of(self.g.z * self.own, 8), self.own)]
        for d in range(self.g.outer - 1):
            total = total + self.r2[d]
        at = pl.multiple_of(base + self.half_at(self.g.x) + self.g.z * self.own, 8)
        rows = pl.ds(at, self.own)
        new[rows] = old[rows] * total / mass()
        for d in range(1, self.g.outer):
            self.copy(new.at[rows], new.at[rows], 2, self.g.peer(d)).start()

    def s4(self):
        if self.g.outer > 1:
            self.many(self.recv.at[2])
            self.many(self.send.at[1])
        rows = pl.ds(pl.multiple_of(self.base + self.half_at(self.g.x), 8), self.half)
        self.c4 = self.copy(self.new.at[rows], self.new.at[rows], 3, self.g.pair)
        self.c4.start()

    def s5(self):
        self.c4.wait()
        if self.g.outer > 1:
            self.many(self.send.at[2])


class Mass:
    def __init__(self, group, buf, got, send, recv):
        self.g, self.buf, self.got, self.send, self.recv = group, buf, got, send, recv

    def copy(self, src, dst, stage, device):
        return pltpu.make_async_remote_copy(
            src_ref=src, dst_ref=dst, send_sem=self.send.at[stage], recv_sem=self.recv.at[stage],
            device_id=device, device_id_type=MESH)

    def s1(self, value):
        self.buf[0] = value
        self.c1 = self.copy(self.buf.at[0], self.got.at[0], 0, self.g.pair)
        self.c1.start()

    def s2(self):
        self.c1.wait()
        self.buf[1] = self.buf[0] + self.got[0]
        for d in range(1, self.g.outer):
            self.copy(self.buf.at[1], self.got.at[d], 1, self.g.peer(d)).start()

    def s3(self):
        total = self.buf[1]
        if self.g.outer > 1:
            rest = self.got.at[pl.ds(1, self.g.outer - 1)]
            pltpu.make_async_copy(rest, rest, self.recv.at[1]).wait()
            pltpu.make_async_copy(rest, rest, self.send.at[1]).wait()
            for d in range(1, self.g.outer):
                total = total + self.got[d]
        self.buf[2] = jnp.broadcast_to(jnp.sum(total, axis=0, keepdims=True), total.shape)

    def value(self):
        return self.buf[2, 0:1]


def kernel(docs_axis, terms_axis, doc_chunks, term_chunks, slab, h_in, w_in, h_out, w_out,
           hbuf, wbuf, wk, tt,
           dpart, dr1, dacc, dr2, dsend, drecv,
           tpart, tr1, tacc, tr2, tsend, trecv,
           mbuf, mgot, msend, mrecv, cbuf, cgot, csend, crecv):
    docs, terms = slab.shape
    rank = h_in.shape[1]
    gt, gd = Group(*terms_axis), Group(*docs_axis)
    peers = gt.everyone() + gd.everyone()
    barrier = pltpu.get_barrier_semaphore()
    for device in peers:
        pl.semaphore_signal(barrier, inc=1, device_id=device, device_id_type=MESH)
    pl.semaphore_wait(barrier, len(peers))

    chunk, tchunk = docs // doc_chunks, terms // term_chunks

    def split_terms(w, t):
        rows = slice(t * tchunk, (t + 1) * tchunk)
        high, low = halves(w)
        wk[rows, :rank] = high
        wk[rows, rank:2 * rank] = high
        wk[rows, 2 * rank:] = low

    def quotients(h, c, t):
        high, low = halves(h)
        lhs = jnp.concatenate([high, low, high], axis=1)
        rows, cols = slice(c * chunk, (c + 1) * chunk), slice(t * tchunk, (t + 1) * tchunk)
        product = dot(lhs, wk[cols], ((1,), (1,)))
        return halves(slab[rows, cols] / product)

    def doc_partial(h, c, tiles, out):
        both, one = None, None
        for t in tiles:
            high, low = quotients(h, c, t)
            cols = slice(t * tchunk, (t + 1) * tchunk)
            b = dot(high, wk[cols, rank:])
            o = dot(low, wk[cols, :rank])
            both, one = (b, o) if both is None else (both + b, one + o)
        value = both[:, :rank] + both[:, rank:] + one
        out[...] = value if tiles[0] == 0 else out[...] + value

    def term_partial(h, c, t):
        high_t, low_t = halves(h.T)
        lhs = jnp.concatenate([high_t, low_t, high_t], axis=1)
        high, low = quotients(h, c, t)
        value = dot(lhs, jnp.concatenate([high, high, low], axis=0))
        cols = slice(t * tchunk, (t + 1) * tchunk)
        if c > 0:
            value = value + tt[:, cols]
        if c < doc_chunks - 1:
            tt[:, cols] = value
        return value

    def w_ref(o):
        if o == 0:
            return w_in
        return w_out if o == OUTER else wbuf.at[o - 1]

    def h_ref(u):
        if u == 0:
            return h_in
        return h_out if u == OUTER * INNER else hbuf.at[u - 1]

    tiles = list(range(term_chunks))
    count = INNER * doc_chunks
    lag = max(doc_chunks // 4, 1)
    for t in tiles:
        split_terms(w_in[t * tchunk:(t + 1) * tchunk], t)
    term_mass = fold(w_in[...])
    for o in range(OUTER):
        mass = Mass(gt, mbuf.at[o], mgot.at[o], msend.at[o], mrecv.at[o])
        mass.s1(term_mass)
        sums = Mass(gd, cbuf.at[o], cgot.at[o], csend.at[o], crecv.at[o])

        jobs, term_jobs = [], []
        doc_mass = None
        for j in range(count + doc_chunks):
            u, c = o * INNER + j // doc_chunks, j % doc_chunks
            if j >= doc_chunks:
                jobs[j - doc_chunks].s5()
            h = h_ref(u)[c * chunk:(c + 1) * chunk]
            if j < count:
                doc_partial(h, c, tiles[-1:] if o > 0 and j < doc_chunks else tiles, dpart.at[u, c])
                job = Reduce(gt, chunk, dpart.at[u, c], dr1.at[u, c], dacc.at[u, c], dr2.at[u, c],
                             dsend.at[u, c], drecv.at[u, c])
                job.u, job.c = u, c
                jobs.append(job)
                job.s1()
            else:
                doc_mass = fold(h) if doc_mass is None else doc_mass + fold(h)
                if c == doc_chunks - 1:
                    sums.s1(doc_mass)
                for t in tiles:
                    value = term_partial(h, c, t)
                    if c == doc_chunks - 1:
                        tpart[o, t] = value.T
                        job = Reduce(gd, tchunk, tpart.at[o, t], tr1.at[o, t], tacc.at[o, t], tr2.at[o, t],
                                     tsend.at[o, t], trecv.at[o, t])
                        term_jobs.append(job)
                        job.s1()
            if j == 1:
                mass.s2()
            if j == 2:
                mass.s3()
            if 0 <= j - lag < count:
                jobs[j - lag].s2()
            if 0 <= j - 2 * lag < count:
                k = jobs[j - 2 * lag]
                k.s3(k.c * chunk, h_ref(k.u), h_ref(k.u + 1), mass.value)
            if 0 <= j - 3 * lag < count:
                jobs[j - 3 * lag].s4()

        sums.s2()
        for job in term_jobs:
            job.s2()
        sums.s3()
        for t, job in enumerate(term_jobs):
            job.s3(t * tchunk, w_ref(o), w_ref(o + 1), sums.value)
        for job in term_jobs:
            job.s4()
        term_mass = None
        for t, job in enumerate(term_jobs):
            job.s5()
            if o == OUTER - 1:
                continue
            w = w_ref(o + 1)[t * tchunk:(t + 1) * tchunk]
            term_mass = fold(w) if term_mass is None else term_mass + fold(w)
            split_terms(w, t)
            if t < term_chunks - 1:
                u = (o + 1) * INNER
                for c in range(doc_chunks):
                    doc_partial(h_ref(u)[c * chunk:(c + 1) * chunk], c, [t], dpart.at[u, c])


def solution(mesh):
    n, m = mesh.shape["term"], mesh.shape["doc"]

    def on_device(slab, h, w):
        docs, rank = h.shape
        terms = w.shape[0]
        doc_chunks = min(DOC_CHUNKS, docs // (8 * n))
        term_chunks = min(TERM_CHUNKS, terms // (8 * m))
        chunk, tchunk = docs // doc_chunks, terms // term_chunks
        vmem = pl.BlockSpec(memory_space=pltpu.VMEM)
        updates = OUTER * INNER

        def reduce_scratch(lead, rows, size):
            outer = size // 2
            half = rows // 2
            return [
                pltpu.VMEM(lead + (rows, rank), F32),
                pltpu.VMEM(lead + (half, rank), F32),
                pltpu.VMEM(lead + (half, rank), F32),
                pltpu.VMEM(lead + (max(outer - 1, 1), half // outer, rank), F32),
                pltpu.SemaphoreType.DMA(lead + (4,)),
                pltpu.SemaphoreType.DMA(lead + (4,)),
            ]

        def mass_scratch(size):
            return [
                pltpu.VMEM((OUTER, 3, 8, rank), F32),
                pltpu.VMEM((OUTER, size // 2, 8, rank), F32),
                pltpu.SemaphoreType.DMA((OUTER, 2)),
                pltpu.SemaphoreType.DMA((OUTER, 2)),
            ]

        return pl.pallas_call(
            functools.partial(kernel, ("doc", m), ("term", n), doc_chunks, term_chunks),
            out_shape=[jax.ShapeDtypeStruct(h.shape, F32), jax.ShapeDtypeStruct(w.shape, F32)],
            in_specs=[vmem] * 3,
            out_specs=[vmem] * 2,
            scratch_shapes=[
                pltpu.VMEM((updates - 1, docs, rank), F32),
                pltpu.VMEM((max(OUTER - 1, 1), terms, rank), F32),
                pltpu.VMEM((terms, 3 * rank), BF16),
                pltpu.VMEM((rank, terms), F32),
                *reduce_scratch((updates, doc_chunks), chunk, n),
                *reduce_scratch((OUTER, term_chunks), tchunk, m),
                *mass_scratch(n),
                *mass_scratch(m),
            ],
            compiler_params=pltpu.CompilerParams(
                collective_id=0, has_side_effects=True, vmem_limit_bytes=56 * 1024 * 1024),
            cost_estimate=pl.CostEstimate(
                flops=36 * 2 * docs * terms * rank, bytes_accessed=6 * docs * terms, transcendentals=0),
        )(slab, h, w)

    return jax.shard_map(
        on_device,
        mesh=mesh,
        in_specs=(P("doc", "term"), P("doc", None), P("term", None)),
        out_specs=(P("doc", None), P("term", None)),
        check_vma=False,
    )
```

```python
import functools

import jax
import jax.numpy as jnp
from jax import lax
from jax.experimental import pallas as pl
from jax.experimental.pallas import tpu as pltpu
from jax.sharding import PartitionSpec as P

OUTER = 2
INNER = 2
DOC_CHUNKS = 4
TERM_CHUNKS = 4
MESH = pl.DeviceIdType.MESH
F32 = jnp.float32
BF16 = jnp.bfloat16


def halves(x):
    high = x.astype(BF16)
    return high, (x - high.astype(F32)).astype(BF16)


def dot(a, b, dims=((1,), (0,))):
    return lax.dot_general(a, b, (dims, ((), ())), preferred_element_type=F32)


def inverse(x):
    y = pl.reciprocal(x, approx=True)
    return y * (2.0 - x * y)


def fold(x):
    rows, cols = x.shape
    return jnp.sum(x.reshape(rows // 8, 8, cols), axis=0)


class Group:
    def __init__(self, axis, size, inner):
        self.axis, self.inner = axis, inner
        self.outer = size // inner
        self.me = lax.axis_index(axis)
        self.x = lax.rem(self.me, inner)
        self.z = lax.div(self.me, inner)
        self.pair = {axis: self.me + 1 - 2 * self.x} if inner == 2 else None

    def place(self, d):
        return lax.rem(self.z + d, self.outer)

    def peer(self, d):
        return {self.axis: self.place(d) * self.inner + self.x}

    def everyone(self):
        return ([self.pair] if self.pair else []) + [self.peer(d) for d in range(1, self.outer)]


class Reduce:
    def __init__(self, group, rows, part, r1, acc, r2, send, recv):
        self.g, self.rows = group, rows
        self.half = rows // group.inner
        self.own = self.half // group.outer
        self.part, self.r1, self.acc, self.r2 = part, r1, acc, r2
        self.send, self.recv = send, recv

    def copy(self, src, dst, stage, device):
        return pltpu.make_async_remote_copy(
            src_ref=src, dst_ref=dst, send_sem=self.send.at[stage], recv_sem=self.recv.at[stage],
            device_id=device, device_id_type=MESH)

    def many(self, sem):
        pltpu.make_async_copy(self.r2, self.r2, sem).wait()

    def half_at(self, x):
        return pl.multiple_of(x * self.half, 8)

    def s1(self):
        if self.g.inner == 1:
            self.acc = self.part
            self.scatter()
            return
        self.c1 = self.copy(self.part.at[pl.ds(self.half_at(1 - self.g.x), self.half)], self.r1, 0, self.g.pair)
        self.c1.start()

    def s2(self):
        if self.g.inner == 1:
            return
        self.c1.wait()
        self.acc[...] = self.part[pl.ds(self.half_at(self.g.x), self.half)] + self.r1[...]
        self.scatter()

    def scatter(self):
        for d in range(1, self.g.outer):
            at = pl.multiple_of(self.g.place(d) * self.own, 8)
            self.copy(self.acc.at[pl.ds(at, self.own)], self.r2.at[d - 1], 1, self.g.peer(d)).start()

    def s3(self, base, old, new, mass):
        self.new, self.base = new, base
        if self.g.outer > 1:
            self.many(self.recv.at[1])
        total = self.acc[pl.ds(pl.multiple_of(self.g.z * self.own, 8), self.own)]
        for d in range(self.g.outer - 1):
            total = total + self.r2[d]
        at = pl.multiple_of(base + self.half_at(self.g.x) + self.g.z * self.own, 8)
        rows = pl.ds(at, self.own)
        new[rows] = old[rows] * total / mass()
        for d in range(1, self.g.outer):
            self.copy(new.at[rows], new.at[rows], 2, self.g.peer(d)).start()

    def s4(self):
        if self.g.inner == 1:
            return
        if self.g.outer > 1:
            self.many(self.recv.at[2])
            self.many(self.send.at[1])
        rows = pl.ds(pl.multiple_of(self.base + self.half_at(self.g.x), 8), self.half)
        self.c4 = self.copy(self.new.at[rows], self.new.at[rows], 3, self.g.pair)
        self.c4.start()

    def s5(self):
        if self.g.inner == 2:
            self.c4.wait()
        else:
            self.many(self.recv.at[2])
            self.many(self.send.at[1])
        if self.g.outer > 1:
            self.many(self.send.at[2])


class Mass:
    def __init__(self, group, buf, got, send, recv):
        self.g, self.buf, self.got, self.send, self.recv = group, buf, got, send, recv

    def copy(self, src, dst, stage, device):
        return pltpu.make_async_remote_copy(
            src_ref=src, dst_ref=dst, send_sem=self.send.at[stage], recv_sem=self.recv.at[stage],
            device_id=device, device_id_type=MESH)

    def s1(self, value):
        self.buf[0] = value
        if self.g.inner == 1:
            self.buf[1] = value
            self.scatter()
            return
        self.c1 = self.copy(self.buf.at[0], self.got.at[0], 0, self.g.pair)
        self.c1.start()

    def s2(self):
        if self.g.inner == 1:
            return
        self.c1.wait()
        self.buf[1] = self.buf[0] + self.got[0]
        self.scatter()

    def scatter(self):
        for d in range(1, self.g.outer):
            self.copy(self.buf.at[1], self.got.at[d], 1, self.g.peer(d)).start()

    def s3(self):
        total = self.buf[1]
        if self.g.outer > 1:
            rest = self.got.at[pl.ds(1, self.g.outer - 1)]
            pltpu.make_async_copy(rest, rest, self.recv.at[1]).wait()
            pltpu.make_async_copy(rest, rest, self.send.at[1]).wait()
            for d in range(1, self.g.outer):
                total = total + self.got[d]
        self.buf[2] = jnp.broadcast_to(jnp.sum(total, axis=0, keepdims=True), total.shape)

    def value(self):
        return self.buf[2, 0:1]


def kernel(docs_axis, terms_axis, doc_chunks, term_chunks, slab, h_in, w_in, h_out, w_out,
           hbuf, wbuf, wk, tt,
           dpart, dr1, dacc, dr2, dsend, drecv,
           tpart, tr1, tacc, tr2, tsend, trecv,
           mbuf, mgot, msend, mrecv, cbuf, cgot, csend, crecv):
    docs, terms = slab.shape
    rank = h_in.shape[1]
    gt, gd = Group(*terms_axis, 1), Group(*docs_axis, 2)
    peers = gt.everyone() + gd.everyone()
    barrier = pltpu.get_barrier_semaphore()
    for device in peers:
        pl.semaphore_signal(barrier, inc=1, device_id=device, device_id_type=MESH)
    pl.semaphore_wait(barrier, len(peers))

    chunk, tchunk = docs // doc_chunks, terms // term_chunks

    def split_terms(w, t):
        rows = slice(t * tchunk, (t + 1) * tchunk)
        high, low = halves(w)
        wk[rows, :rank] = high
        wk[rows, rank:2 * rank] = high
        wk[rows, 2 * rank:] = low

    def quotients(h, c, t):
        high, low = halves(h)
        lhs = jnp.concatenate([high, low, high], axis=1)
        rows, cols = slice(c * chunk, (c + 1) * chunk), slice(t * tchunk, (t + 1) * tchunk)
        product = dot(lhs, wk[cols], ((1,), (1,)))
        return halves(slab[rows, cols] * inverse(product))

    def doc_partial(h, c, tiles, out):
        both, one = None, None
        for t in tiles:
            high, low = quotients(h, c, t)
            cols = slice(t * tchunk, (t + 1) * tchunk)
            b = dot(high, wk[cols, rank:])
            o = dot(low, wk[cols, :rank])
            both, one = (b, o) if both is None else (both + b, one + o)
        value = both[:, :rank] + both[:, rank:] + one
        out[...] = value if tiles[0] == 0 else out[...] + value

    def term_partial(h, c, t):
        high_t, low_t = halves(h.T)
        lhs = jnp.concatenate([high_t, low_t, high_t], axis=1)
        high, low = quotients(h, c, t)
        value = dot(lhs, jnp.concatenate([high, high, low], axis=0))
        cols = slice(t * tchunk, (t + 1) * tchunk)
        if c > 0:
            value = value + tt[:, cols]
        if c < doc_chunks - 1:
            tt[:, cols] = value
        return value

    def w_ref(o):
        if o == 0:
            return w_in
        return w_out if o == OUTER else wbuf.at[o - 1]

    def h_ref(u):
        if u == 0:
            return h_in
        return h_out if u == OUTER * INNER else hbuf.at[u - 1]

    tiles = list(range(term_chunks))
    count = INNER * doc_chunks
    lag = max(doc_chunks // 2, 1)
    for t in tiles:
        split_terms(w_in[t * tchunk:(t + 1) * tchunk], t)
    term_mass = fold(w_in[...])
    for o in range(OUTER):
        mass = Mass(gt, mbuf.at[o], mgot.at[o], msend.at[o], mrecv.at[o])
        mass.s1(term_mass)
        sums = Mass(gd, cbuf.at[o], cgot.at[o], csend.at[o], crecv.at[o])

        jobs, term_jobs = [], []
        doc_mass = None
        for j in range(count + doc_chunks):
            u, c = o * INNER + j // doc_chunks, j % doc_chunks
            if j >= doc_chunks:
                jobs[j - doc_chunks].s5()
            h = h_ref(u)[c * chunk:(c + 1) * chunk]
            if j < count:
                doc_partial(h, c, tiles[-1:] if o > 0 and j < doc_chunks else tiles, dpart.at[u, c])
                job = Reduce(gt, chunk, dpart.at[u, c], dr1.at[u, c], dacc.at[u, c], dr2.at[u, c],
                             dsend.at[u, c], drecv.at[u, c])
                job.u, job.c = u, c
                jobs.append(job)
                job.s1()
            else:
                doc_mass = fold(h) if doc_mass is None else doc_mass + fold(h)
                if c == doc_chunks - 1:
                    sums.s1(doc_mass)
                for t in tiles:
                    value = term_partial(h, c, t)
                    if c == doc_chunks - 1:
                        tpart[o, t] = value.T
                        job = Reduce(gd, tchunk, tpart.at[o, t], tr1.at[o, t], tacc.at[o, t], tr2.at[o, t],
                                     tsend.at[o, t], trecv.at[o, t])
                        term_jobs.append(job)
                        job.s1()
            if j == 1:
                mass.s3()
            if 0 <= j - lag < count:
                k = jobs[j - lag]
                k.s3(k.c * chunk, h_ref(k.u), h_ref(k.u + 1), mass.value)

        sums.s2()
        for job in term_jobs:
            job.s2()
        sums.s3()
        for t, job in enumerate(term_jobs):
            job.s3(t * tchunk, w_ref(o), w_ref(o + 1), sums.value)
        for job in term_jobs:
            job.s4()
        term_mass = None
        for t, job in enumerate(term_jobs):
            job.s5()
            if o == OUTER - 1:
                continue
            w = w_ref(o + 1)[t * tchunk:(t + 1) * tchunk]
            term_mass = fold(w) if term_mass is None else term_mass + fold(w)
            split_terms(w, t)
            if t < term_chunks - 1:
                u = (o + 1) * INNER
                for c in range(doc_chunks):
                    doc_partial(h_ref(u)[c * chunk:(c + 1) * chunk], c, [t], dpart.at[u, c])


def solution(mesh):
    n, m = mesh.shape["term"], mesh.shape["doc"]

    def on_device(slab, h, w):
        docs, rank = h.shape
        terms = w.shape[0]
        doc_chunks = min(DOC_CHUNKS, docs // (8 * n))
        term_chunks = min(TERM_CHUNKS, terms // (8 * m))
        chunk, tchunk = docs // doc_chunks, terms // term_chunks
        vmem = pl.BlockSpec(memory_space=pltpu.VMEM)
        updates = OUTER * INNER

        def reduce_scratch(lead, rows, size, inner):
            outer, half = size // inner, rows // inner
            near = half if inner == 2 else 8
            return [
                pltpu.VMEM(lead + (rows, rank), F32),
                pltpu.VMEM(lead + (near, rank), F32),
                pltpu.VMEM(lead + (near, rank), F32),
                pltpu.VMEM(lead + (max(outer - 1, 1), half // outer, rank), F32),
                pltpu.SemaphoreType.DMA(lead + (4,)),
                pltpu.SemaphoreType.DMA(lead + (4,)),
            ]

        def mass_scratch(size, inner):
            return [
                pltpu.VMEM((OUTER, 3, 8, rank), F32),
                pltpu.VMEM((OUTER, size // inner, 8, rank), F32),
                pltpu.SemaphoreType.DMA((OUTER, 2)),
                pltpu.SemaphoreType.DMA((OUTER, 2)),
            ]

        return pl.pallas_call(
            functools.partial(kernel, ("doc", m), ("term", n), doc_chunks, term_chunks),
            out_shape=[jax.ShapeDtypeStruct(h.shape, F32), jax.ShapeDtypeStruct(w.shape, F32)],
            in_specs=[vmem] * 3,
            out_specs=[vmem] * 2,
            scratch_shapes=[
                pltpu.VMEM((updates - 1, docs, rank), F32),
                pltpu.VMEM((max(OUTER - 1, 1), terms, rank), F32),
                pltpu.VMEM((terms, 3 * rank), BF16),
                pltpu.VMEM((rank, terms), F32),
                *reduce_scratch((updates, doc_chunks), chunk, n, 1),
                *reduce_scratch((OUTER, term_chunks), tchunk, m, 2),
                *mass_scratch(n, 1),
                *mass_scratch(m, 2),
            ],
            compiler_params=pltpu.CompilerParams(
                collective_id=0, has_side_effects=True, vmem_limit_bytes=56 * 1024 * 1024),
            cost_estimate=pl.CostEstimate(
                flops=36 * 2 * docs * terms * rank, bytes_accessed=6 * docs * terms, transcendentals=0),
        )(slab, h, w)

    return jax.shard_map(
        on_device,
        mesh=mesh,
        in_specs=(P("doc", "term"), P("doc", None), P("term", None)),
        out_specs=(P("doc", None), P("term", None)),
        check_vma=False,
    )
```

```python
import functools

import jax
import jax.numpy as jnp
from jax import lax
from jax.experimental import pallas as pl
from jax.experimental.pallas import tpu as pltpu
from jax.sharding import PartitionSpec as P

OUTER = 2
INNER = 2
DOC_CHUNKS = 8
TERM_CHUNKS = 4
MESH = pl.DeviceIdType.MESH
F32 = jnp.float32
BF16 = jnp.bfloat16


def halves(x):
    high = x.astype(BF16)
    return high, (x - high.astype(F32)).astype(BF16)


def dot(a, b, dims=((1,), (0,))):
    return lax.dot_general(a, b, (dims, ((), ())), preferred_element_type=F32)


def inverse(x):
    y = pl.reciprocal(x, approx=True)
    return y * (2.0 - x * y)


def fold(x):
    rows, cols = x.shape
    return jnp.sum(x.reshape(rows // 8, 8, cols), axis=0)


class Group:
    def __init__(self, axis, size):
        self.axis, self.size = axis, size
        self.outer = size // 2
        self.me = lax.axis_index(axis)
        self.x = lax.rem(self.me, 2)
        self.z = lax.div(self.me, 2)
        self.pair = {axis: self.me + 1 - 2 * self.x}

    def place(self, d):
        return lax.rem(self.z + d, self.outer)

    def peer(self, d):
        return {self.axis: self.place(d) * 2 + self.x}

    def everyone(self):
        return [self.pair] + [self.peer(d) for d in range(1, self.outer)]


class Reduce:
    def __init__(self, group, rows, scratch, index, base, old, new):
        self.g, self.rows, self.base, self.old, self.new = group, rows, base, old, new
        self.half, self.own = rows // 2, rows // 2 // group.outer
        self.part, self.r1, self.acc, self.r2, self.send, self.recv = [ref.at[index] for ref in scratch]

    def copy(self, src, dst, stage, device):
        return pltpu.make_async_remote_copy(
            src_ref=src, dst_ref=dst, send_sem=self.send.at[stage], recv_sem=self.recv.at[stage],
            device_id=device, device_id_type=MESH)

    def many(self, sem):
        pltpu.make_async_copy(self.r2, self.r2, sem).wait()

    def half_at(self, x):
        return pl.multiple_of(x * self.half, 8)

    def near(self):
        return self.copy(self.part.at[pl.ds(self.half_at(1 - self.g.x), self.half)], self.r1, 0, self.g.pair)

    def back(self):
        rows = pl.ds(pl.multiple_of(self.base + self.half_at(self.g.x), 8), self.half)
        return self.copy(self.new.at[rows], self.new.at[rows], 3, self.g.pair)

    def s1(self):
        self.near().start()

    def s2(self):
        self.near().wait()
        self.acc[...] = self.part[pl.ds(self.half_at(self.g.x), self.half)] + self.r1[...]
        for d in range(1, self.g.outer):
            at = pl.multiple_of(self.g.place(d) * self.own, 8)
            self.copy(self.acc.at[pl.ds(at, self.own)], self.r2.at[d - 1], 1, self.g.peer(d)).start()

    def s3(self, mass):
        if self.g.outer > 1:
            self.many(self.recv.at[1])
        total = self.acc[pl.ds(pl.multiple_of(self.g.z * self.own, 8), self.own)]
        for d in range(self.g.outer - 1):
            total = total + self.r2[d]
        at = pl.multiple_of(self.base + self.half_at(self.g.x) + self.g.z * self.own, 8)
        rows = pl.ds(at, self.own)
        self.new[rows] = self.old[rows] * total / mass()
        for d in range(1, self.g.outer):
            self.copy(self.new.at[rows], self.new.at[rows], 2, self.g.peer(d)).start()

    def s4(self):
        if self.g.outer > 1:
            self.many(self.recv.at[2])
            self.many(self.send.at[1])
        self.back().start()

    def s5(self):
        self.back().wait()
        if self.g.outer > 1:
            self.many(self.send.at[2])


class Mass:
    def __init__(self, group, buf, got, send, recv):
        self.g, self.buf, self.got, self.send, self.recv = group, buf, got, send, recv

    def copy(self, src, dst, stage, device):
        return pltpu.make_async_remote_copy(
            src_ref=src, dst_ref=dst, send_sem=self.send.at[stage], recv_sem=self.recv.at[stage],
            device_id=device, device_id_type=MESH)

    def s1(self, value):
        self.buf[0] = value
        self.near().start()

    def near(self):
        return self.copy(self.buf.at[0], self.got.at[0], 0, self.g.pair)

    def s2(self):
        self.near().wait()
        self.buf[1] = self.buf[0] + self.got[0]
        for d in range(1, self.g.outer):
            self.copy(self.buf.at[1], self.got.at[d], 1, self.g.peer(d)).start()

    def s3(self):
        total = self.buf[1]
        if self.g.outer > 1:
            rest = self.got.at[pl.ds(1, self.g.outer - 1)]
            pltpu.make_async_copy(rest, rest, self.recv.at[1]).wait()
            pltpu.make_async_copy(rest, rest, self.send.at[1]).wait()
            for d in range(1, self.g.outer):
                total = total + self.got[d]
        self.buf[2] = jnp.broadcast_to(jnp.sum(total, axis=0, keepdims=True), total.shape)

    def value(self):
        return self.buf[2, 0:1]


def kernel(docs_axis, terms_axis, doc_chunks, term_chunks, slab, h_in, w_in, h_out, w_out,
           hbuf, wbuf, wt, wk, tt, dm,
           dpart, dr1, dacc, dr2, dsend, drecv,
           tpart, tr1, tacc, tr2, tsend, trecv,
           mbuf, mgot, msend, mrecv, cbuf, cgot, csend, crecv):
    docs, terms = slab.shape
    rank = h_in.shape[1]
    gt, gd = Group(*terms_axis), Group(*docs_axis)
    peers = gt.everyone() + gd.everyone()
    barrier = pltpu.get_barrier_semaphore()
    for device in peers:
        pl.semaphore_signal(barrier, inc=1, device_id=device, device_id_type=MESH)
    pl.semaphore_wait(barrier, len(peers))

    chunk, tchunk = docs // doc_chunks, terms // term_chunks

    tiles = [slice(t * tchunk, (t + 1) * tchunk) for t in range(term_chunks)]

    def quotients(h, rows, cols):
        high, low = halves(h)
        lhs = jnp.concatenate([high, low, high], axis=1)
        return halves(slab[rows, cols] * inverse(dot(lhs, wt[:, cols])))

    def doc_partial(h, rows, out):
        both, one = None, None
        for cols in tiles:
            high, low = quotients(h, rows, cols)
            b = dot(high, wk[cols])
            o = dot(low, wk[cols, :rank])
            both, one = (b, o) if both is None else (both + b, one + o)
        out[...] = both[:, :rank] + both[:, rank:] + one

    def term_partial(h, rows):
        high_t, low_t = halves(h.T)
        lhs = jnp.concatenate([high_t, low_t, high_t], axis=1)
        for cols in tiles:
            high, low = quotients(h, rows, cols)
            tt[:, cols] += dot(lhs, jnp.concatenate([high, high, low], axis=0))

    count = INNER * doc_chunks
    lag = max(doc_chunks // 4, 1)
    hbuf[0] = h_in[...]
    wbuf[0] = w_in[...]

    def doc_job(q):
        u, c = lax.div(q, doc_chunks), lax.rem(q, doc_chunks)
        return Reduce(gt, chunk, (dpart, dr1, dacc, dr2, dsend, drecv), (u, c), c * chunk, hbuf.at[u], hbuf.at[u + 1])

    def outer(o, carry):
        mass = Mass(gt, mbuf.at[o], mgot.at[o], msend.at[o], mrecv.at[o])
        sums = Mass(gd, cbuf.at[o], cgot.at[o], csend.at[o], crecv.at[o])
        w_now, w_next = wbuf.at[o], wbuf.at[o + 1]
        mass.s1(fold(w_now[...]))
        for cols in tiles:
            high, low = halves(w_now[cols])
            wk[cols, :rank] = high
            wk[cols, rank:] = low
            high, low = halves(w_now[cols].T)
            wt[:rank, cols] = high
            wt[rank:2 * rank, cols] = high
            wt[2 * rank:, cols] = low
        tt[...] = jnp.zeros_like(tt)
        dm[...] = jnp.zeros_like(dm)

        def tick(j, carry):
            q = o * count + j
            u, c = lax.div(q, doc_chunks), lax.rem(q, doc_chunks)
            rows = pl.ds(pl.multiple_of(c * chunk, 8), chunk)

            @pl.when(j >= doc_chunks)
            def _():
                doc_job(q - doc_chunks).s5()

            @pl.when(j < count)
            def _():
                doc_partial(hbuf[u, rows], rows, dpart.at[u, c])
                doc_job(q).s1()

            @pl.when(j >= count)
            def _():
                h = hbuf[u, rows]
                dm[...] += fold(h)
                term_partial(h, rows)

            @pl.when(j == 1)
            def _():
                mass.s2()

            @pl.when(j == 2)
            def _():
                mass.s3()

            @pl.when(jnp.logical_and(j >= lag, j < count + lag))
            def _():
                doc_job(q - lag).s2()

            @pl.when(jnp.logical_and(j >= 2 * lag, j < count + 2 * lag))
            def _():
                doc_job(q - 2 * lag).s3(mass.value)

            @pl.when(jnp.logical_and(j >= 3 * lag, j < count + 3 * lag))
            def _():
                doc_job(q - 3 * lag).s4()

            return carry

        lax.fori_loop(0, count + doc_chunks, tick, 0)

        sums.s1(dm[...])
        jobs = []
        for t, cols in enumerate(tiles):
            tpart[o, t] = tt[:, cols].T
            jobs.append(Reduce(gd, tchunk, (tpart, tr1, tacc, tr2, tsend, trecv), (o, t), t * tchunk, w_now, w_next))
            jobs[-1].s1()
        sums.s2()
        for job in jobs:
            job.s2()
        sums.s3()
        for job in jobs:
            job.s3(sums.value)
        for job in jobs:
            job.s4()
        for job in jobs:
            job.s5()
        return carry

    lax.fori_loop(0, OUTER, outer, 0)
    h_out[...] = hbuf[OUTER * INNER]
    w_out[...] = wbuf[OUTER]


def solution(mesh):
    n, m = mesh.shape["term"], mesh.shape["doc"]

    def on_device(slab, h, w):
        docs, rank = h.shape
        terms = w.shape[0]
        doc_chunks = min(DOC_CHUNKS, docs // (8 * n))
        term_chunks = min(TERM_CHUNKS, terms // (8 * m))
        chunk, tchunk = docs // doc_chunks, terms // term_chunks
        vmem = pl.BlockSpec(memory_space=pltpu.VMEM)
        updates = OUTER * INNER

        def reduce_scratch(lead, rows, size):
            outer = size // 2
            half = rows // 2
            return [
                pltpu.VMEM(lead + (rows, rank), F32),
                pltpu.VMEM(lead + (half, rank), F32),
                pltpu.VMEM(lead + (half, rank), F32),
                pltpu.VMEM(lead + (max(outer - 1, 1), half // outer, rank), F32),
                pltpu.SemaphoreType.DMA(lead + (4,)),
                pltpu.SemaphoreType.DMA(lead + (4,)),
            ]

        def mass_scratch(size):
            return [
                pltpu.VMEM((OUTER, 3, 8, rank), F32),
                pltpu.VMEM((OUTER, size // 2, 8, rank), F32),
                pltpu.SemaphoreType.DMA((OUTER, 2)),
                pltpu.SemaphoreType.DMA((OUTER, 2)),
            ]

        return pl.pallas_call(
            functools.partial(kernel, ("doc", m), ("term", n), doc_chunks, term_chunks),
            out_shape=[jax.ShapeDtypeStruct(h.shape, F32), jax.ShapeDtypeStruct(w.shape, F32)],
            in_specs=[vmem] * 3,
            out_specs=[vmem] * 2,
            scratch_shapes=[
                pltpu.VMEM((updates + 1, docs, rank), F32),
                pltpu.VMEM((OUTER + 1, terms, rank), F32),
                pltpu.VMEM((3 * rank, terms), BF16),
                pltpu.VMEM((terms, 2 * rank), BF16),
                pltpu.VMEM((rank, terms), F32),
                pltpu.VMEM((8, rank), F32),
                *reduce_scratch((updates, doc_chunks), chunk, n),
                *reduce_scratch((OUTER, term_chunks), tchunk, m),
                *mass_scratch(n),
                *mass_scratch(m),
            ],
            compiler_params=pltpu.CompilerParams(
                collective_id=0, has_side_effects=True, vmem_limit_bytes=56 * 1024 * 1024),
            cost_estimate=pl.CostEstimate(
                flops=36 * 2 * docs * terms * rank, bytes_accessed=6 * docs * terms, transcendentals=0),
        )(slab, h, w)

    return jax.shard_map(
        on_device,
        mesh=mesh,
        in_specs=(P("doc", "term"), P("doc", None), P("term", None)),
        out_specs=(P("doc", None), P("term", None)),
        check_vma=False,
    )
```

```python
import functools

import jax
import jax.numpy as jnp
from jax import lax
from jax.experimental import pallas as pl
from jax.experimental.pallas import tpu as pltpu
from jax.sharding import PartitionSpec as P

OUTER = 2
INNER = 2
DOC_CHUNKS = 8
TERM_CHUNKS = 4
MESH = pl.DeviceIdType.MESH
F32 = jnp.float32
BF16 = jnp.bfloat16


def halves(x):
    high = x.astype(BF16)
    return high, (x - high.astype(F32)).astype(BF16)


def dot(a, b, dims=((1,), (0,))):
    return lax.dot_general(a, b, (dims, ((), ())), preferred_element_type=F32)


def inverse(x):
    y = pl.reciprocal(x, approx=True)
    return y * (2.0 - x * y)


def fold(x):
    rows, cols = x.shape
    return jnp.sum(x.reshape(rows // 8, 8, cols), axis=0)


class Group:
    def __init__(self, axis, size):
        self.axis, self.size = axis, size
        self.outer = size // 2
        self.me = lax.axis_index(axis)
        self.x = lax.rem(self.me, 2)
        self.z = lax.div(self.me, 2)
        self.pair = {axis: self.me + 1 - 2 * self.x}

    def place(self, d):
        return lax.rem(self.z + d, self.outer)

    def peer(self, d):
        return {self.axis: self.place(d) * 2 + self.x}

    def everyone(self):
        return [self.pair] + [self.peer(d) for d in range(1, self.outer)]


class Reduce:
    def __init__(self, group, rows, scratch, index, base, old, new):
        self.g, self.rows, self.base, self.old, self.new = group, rows, base, old, new
        self.half, self.own = rows // 2, rows // 2 // group.outer
        self.part, self.r1, self.acc, self.r2, self.send, self.recv = [ref.at[index] for ref in scratch]

    def copy(self, src, dst, stage, device):
        return pltpu.make_async_remote_copy(
            src_ref=src, dst_ref=dst, send_sem=self.send.at[stage], recv_sem=self.recv.at[stage],
            device_id=device, device_id_type=MESH)

    def many(self, sem):
        pltpu.make_async_copy(self.r2, self.r2, sem).wait()

    def half_at(self, x):
        return pl.multiple_of(x * self.half, 8)

    def near(self):
        return self.copy(self.part.at[pl.ds(self.half_at(1 - self.g.x), self.half)], self.r1, 0, self.g.pair)

    def back(self):
        rows = pl.ds(pl.multiple_of(self.base + self.half_at(self.g.x), 8), self.half)
        return self.copy(self.new.at[rows], self.new.at[rows], 3, self.g.pair)

    def s1(self):
        self.near().start()

    def s2(self):
        self.near().wait()
        self.acc[...] = self.part[pl.ds(self.half_at(self.g.x), self.half)] + self.r1[...]
        for d in range(1, self.g.outer):
            at = pl.multiple_of(self.g.place(d) * self.own, 8)
            self.copy(self.acc.at[pl.ds(at, self.own)], self.r2.at[d - 1], 1, self.g.peer(d)).start()

    def s3(self, mass):
        if self.g.outer > 1:
            self.many(self.recv.at[1])
        total = self.acc[pl.ds(pl.multiple_of(self.g.z * self.own, 8), self.own)]
        for d in range(self.g.outer - 1):
            total = total + self.r2[d]
        at = pl.multiple_of(self.base + self.half_at(self.g.x) + self.g.z * self.own, 8)
        rows = pl.ds(at, self.own)
        self.new[rows] = self.old[rows] * total / mass()
        for d in range(1, self.g.outer):
            self.copy(self.new.at[rows], self.new.at[rows], 2, self.g.peer(d)).start()

    def s4(self):
        if self.g.outer > 1:
            self.many(self.recv.at[2])
            self.many(self.send.at[1])
        self.back().start()

    def s5(self):
        self.back().wait()
        if self.g.outer > 1:
            self.many(self.send.at[2])


class Mass:
    def __init__(self, group, buf, got, send, recv):
        self.g, self.buf, self.got, self.send, self.recv = group, buf, got, send, recv

    def copy(self, src, dst, stage, device):
        return pltpu.make_async_remote_copy(
            src_ref=src, dst_ref=dst, send_sem=self.send.at[stage], recv_sem=self.recv.at[stage],
            device_id=device, device_id_type=MESH)

    def s1(self, value):
        self.buf[0] = value
        self.near().start()

    def near(self):
        return self.copy(self.buf.at[0], self.got.at[0], 0, self.g.pair)

    def s2(self):
        self.near().wait()
        self.buf[1] = self.buf[0] + self.got[0]
        for d in range(1, self.g.outer):
            self.copy(self.buf.at[1], self.got.at[d], 1, self.g.peer(d)).start()

    def s3(self):
        total = self.buf[1]
        if self.g.outer > 1:
            rest = self.got.at[pl.ds(1, self.g.outer - 1)]
            pltpu.make_async_copy(rest, rest, self.recv.at[1]).wait()
            pltpu.make_async_copy(rest, rest, self.send.at[1]).wait()
            for d in range(1, self.g.outer):
                total = total + self.got[d]
        self.buf[2] = jnp.broadcast_to(jnp.sum(total, axis=0, keepdims=True), total.shape)

    def value(self):
        return self.buf[2, 0:1]


def kernel(docs_axis, terms_axis, doc_chunks, term_chunks, slab, h_in, w_in, h_out, w_out,
           hbuf, wbuf, wt, wk, tt, dm,
           dpart, dr1, dacc, dr2, dsend, drecv,
           tpart, tr1, tacc, tr2, tsend, trecv,
           mbuf, mgot, msend, mrecv, cbuf, cgot, csend, crecv):
    docs, terms = slab.shape
    rank = h_in.shape[1]
    gt, gd = Group(*terms_axis), Group(*docs_axis)
    peers = gt.everyone() + gd.everyone()
    barrier = pltpu.get_barrier_semaphore()
    for device in peers:
        pl.semaphore_signal(barrier, inc=1, device_id=device, device_id_type=MESH)
    pl.semaphore_wait(barrier, len(peers))

    chunk, tchunk = docs // doc_chunks, terms // term_chunks

    tiles = [slice(t * tchunk, (t + 1) * tchunk) for t in range(term_chunks)]

    def quotients(h, rows, cols):
        high, low = halves(h)
        lhs = jnp.concatenate([high, low, high], axis=1)
        return halves(slab[rows, cols] * inverse(dot(lhs, wt[:, cols])))

    def doc_partial(h, rows, out):
        total = None
        for cols in tiles:
            high, low = quotients(h, rows, cols)
            both = dot(jnp.concatenate([high, low], axis=0), wk[cols])
            value = both[:chunk, :rank] + (both[:chunk, rank:] + both[chunk:, :rank])
            total = value if total is None else total + value
        out[...] = total

    def term_partial(h, rows):
        high_t, low_t = halves(h.T)
        lhs = jnp.concatenate([high_t, low_t, high_t], axis=1)
        for cols in tiles:
            high, low = quotients(h, rows, cols)
            tt[:, cols] += dot(lhs, jnp.concatenate([high, high, low], axis=0))

    count = INNER * doc_chunks
    lag = max(doc_chunks // 4, 1)
    hbuf[0] = h_in[...]
    wbuf[0] = w_in[...]

    def doc_job(q):
        u, c = lax.div(q, doc_chunks), lax.rem(q, doc_chunks)
        return Reduce(gt, chunk, (dpart, dr1, dacc, dr2, dsend, drecv), (u, c), c * chunk, hbuf.at[u], hbuf.at[u + 1])

    def outer(o, carry):
        mass = Mass(gt, mbuf.at[o], mgot.at[o], msend.at[o], mrecv.at[o])
        sums = Mass(gd, cbuf.at[o], cgot.at[o], csend.at[o], crecv.at[o])
        w_now, w_next = wbuf.at[o], wbuf.at[o + 1]
        mass.s1(fold(w_now[...]))
        for cols in tiles:
            high, low = halves(w_now[cols])
            wk[cols, :rank] = high
            wk[cols, rank:] = low
            high, low = halves(w_now[cols].T)
            wt[:rank, cols] = high
            wt[rank:2 * rank, cols] = high
            wt[2 * rank:, cols] = low
        tt[...] = jnp.zeros_like(tt)
        dm[...] = jnp.zeros_like(dm)

        def tick(j, carry):
            q = o * count + j
            u, c = lax.div(q, doc_chunks), lax.rem(q, doc_chunks)
            rows = pl.ds(pl.multiple_of(c * chunk, 8), chunk)

            @pl.when(j >= doc_chunks)
            def _():
                doc_job(q - doc_chunks).s5()

            @pl.when(j < count)
            def _():
                doc_partial(hbuf[u, rows], rows, dpart.at[u, c])
                doc_job(q).s1()

            @pl.when(j >= count)
            def _():
                h = hbuf[u, rows]
                dm[...] += fold(h)
                term_partial(h, rows)

            @pl.when(j == 1)
            def _():
                mass.s2()

            @pl.when(j == 2)
            def _():
                mass.s3()

            @pl.when(jnp.logical_and(j >= lag, j < count + lag))
            def _():
                doc_job(q - lag).s2()

            @pl.when(jnp.logical_and(j >= 2 * lag, j < count + 2 * lag))
            def _():
                doc_job(q - 2 * lag).s3(mass.value)

            @pl.when(jnp.logical_and(j >= 3 * lag, j < count + 3 * lag))
            def _():
                doc_job(q - 3 * lag).s4()

            return carry

        lax.fori_loop(0, count + doc_chunks, tick, 0)

        sums.s1(dm[...])
        jobs = []
        for t, cols in enumerate(tiles):
            tpart[o, t] = tt[:, cols].T
            jobs.append(Reduce(gd, tchunk, (tpart, tr1, tacc, tr2, tsend, trecv), (o, t), t * tchunk, w_now, w_next))
            jobs[-1].s1()
        sums.s2()
        for job in jobs:
            job.s2()
        sums.s3()
        for job in jobs:
            job.s3(sums.value)
        for job in jobs:
            job.s4()
        for job in jobs:
            job.s5()
        return carry

    lax.fori_loop(0, OUTER, outer, 0)
    h_out[...] = hbuf[OUTER * INNER]
    w_out[...] = wbuf[OUTER]


def hand_over(a, b, a_out, b_out):
    a_out[...] = a[...]
    b_out[...] = b[...]


def solution(mesh):
    n, m = mesh.shape["term"], mesh.shape["doc"]

    def on_device(slab, h, w):
        docs, rank = h.shape
        terms = w.shape[0]
        doc_chunks = min(DOC_CHUNKS, docs // (8 * n))
        term_chunks = min(TERM_CHUNKS, terms // (8 * m))
        chunk, tchunk = docs // doc_chunks, terms // term_chunks
        vmem = pl.BlockSpec(memory_space=pltpu.VMEM)
        updates = OUTER * INNER

        def reduce_scratch(lead, rows, size):
            outer = size // 2
            half = rows // 2
            return [
                pltpu.VMEM(lead + (rows, rank), F32),
                pltpu.VMEM(lead + (half, rank), F32),
                pltpu.VMEM(lead + (half, rank), F32),
                pltpu.VMEM(lead + (max(outer - 1, 1), half // outer, rank), F32),
                pltpu.SemaphoreType.DMA(lead + (4,)),
                pltpu.SemaphoreType.DMA(lead + (4,)),
            ]

        def mass_scratch(size):
            return [
                pltpu.VMEM((OUTER, 3, 8, rank), F32),
                pltpu.VMEM((OUTER, size // 2, 8, rank), F32),
                pltpu.SemaphoreType.DMA((OUTER, 2)),
                pltpu.SemaphoreType.DMA((OUTER, 2)),
            ]

        outs = [jax.ShapeDtypeStruct(h.shape, F32), jax.ShapeDtypeStruct(w.shape, F32)]
        results = pl.pallas_call(
            functools.partial(kernel, ("doc", m), ("term", n), doc_chunks, term_chunks),
            out_shape=outs,
            in_specs=[vmem] * 3,
            out_specs=[vmem] * 2,
            scratch_shapes=[
                pltpu.VMEM((updates + 1, docs, rank), F32),
                pltpu.VMEM((OUTER + 1, terms, rank), F32),
                pltpu.VMEM((3 * rank, terms), BF16),
                pltpu.VMEM((terms, 2 * rank), BF16),
                pltpu.VMEM((rank, terms), F32),
                pltpu.VMEM((8, rank), F32),
                *reduce_scratch((updates, doc_chunks), chunk, n),
                *reduce_scratch((OUTER, term_chunks), tchunk, m),
                *mass_scratch(n),
                *mass_scratch(m),
            ],
            compiler_params=pltpu.CompilerParams(
                collective_id=0, has_side_effects=True, vmem_limit_bytes=56 * 1024 * 1024),
            cost_estimate=pl.CostEstimate(
                flops=36 * 2 * docs * terms * rank, bytes_accessed=6 * docs * terms, transcendentals=0),
        )(slab, h, w)
        return pl.pallas_call(hand_over, out_shape=outs, in_specs=[vmem] * 2, out_specs=[vmem] * 2)(*results)

    return jax.shard_map(
        on_device,
        mesh=mesh,
        in_specs=(P("doc", "term"), P("doc", None), P("term", None)),
        out_specs=(P("doc", None), P("term", None)),
        check_vma=False,
    )
```
